32 devices in a mesh: groups: 2 (over y), rows: 16 (over z, x, core).
Axes of the slice: x: 2, y: 2, z: 4, core: 2. Of those that a mesh axis runs over, the one named last changes fastest.
Arguments:
- images: bfloat16 [2, 256, 256, 256], P(None, ('groups', 'rows')), parts along dimension 1, may hold values from -6 to 6
- third_weight: bfloat16 [3, 3, 256, 256], replicated, may hold values from -0.125 to 0.125
- third_bias: float32 [256], replicated, may hold values from -3 to 3
- fourth_weight: bfloat16 [3, 3, 256, 512], replicated, may hold values from -0.125 to 0.125
- fourth_bias: float32 [512], replicated, may hold values from -3 to 3
- third_linear: float32 [256], replicated, may hold values from 8 to 64
- fourth_linear: float32 [512], replicated, may hold values from 8 to 64
Outputs:
- input_grad: float32 [256, 256, 256], P(('groups', 'rows')), parts along dimension 0
The draws below stay inside these ranges and needn't reach their ends.
There are 2 independent parts, one for each index of `groups`. The reference program is written for one: setup_inputs(seed, part) draws one part's arguments, and reference() takes and returns one part's arrays. A program takes and returns all parts, laid end to end along the dimension named above; an argument that names none is the same for every part. Nothing has to cross between parts.
All inputs are finite; a program needn't handle non-finite values.
Results may differ from the reference program's by a relative error of at most 0.0085.
Values may be sent and summed in bfloat16 or wider, within the bound.
A program may use at most 128 MiB of HBM per device.

```python
import math
import jax
import jax.numpy as jnp
from jax import lax

C3 = 256
C4 = 512
COLS = 256
HEIGHT = 128


def shard_levels(own_key, dims, shards, smallest, top_value):
    def one(position, shards_of):
        heights = jax.random.uniform(jax.random.fold_in(jax.random.fold_in(own_key, 6), position), (shards_of,), jnp.float32, smallest / len(shards), top_value / len(shards))
        return jnp.repeat(jnp.exp(heights), dims[position] // shards_of).reshape((-1,) + (1,) * (len(dims) - position - 1))

    factor_of = one(*shards[0])
    for cut in shards[1:]:
        factor_of = factor_of * one(*cut)
    return factor_of


def scatter_about(own_key, dims, scale, bound, split=(), held_as=jnp.bfloat16):
    loudness = shard_levels(own_key, dims, split, -0.22, 0.18) if split else 1.0
    result = jax.random.normal(own_key, dims, jnp.float32) * scale * loudness
    return jnp.minimum(jnp.maximum(result, -bound), bound).astype(held_as)


def setup_inputs(seed: int = 0, part: int = 0) -> dict:
    streams_of = jax.random.split(jax.random.key(seed), 8)
    part_splits = jax.random.split(jax.random.fold_in(streams_of[7], part), 8)
    return {
        "images": scatter_about(part_splits[0], (2, HEIGHT, COLS, C3), 1.0, 6.0, ((1, 16),)),
        "third_weight": scatter_about(streams_of[1], (3, 3, C3, C3), (9 * C3) ** -0.5, 0.125),
        "third_bias": scatter_about(streams_of[2], (C3,), 0.5, 3.0, (), jnp.float32),
        "fourth_weight": scatter_about(streams_of[3], (3, 3, C3, C4), (9 * C3) ** -0.5, 0.125),
        "fourth_bias": scatter_about(streams_of[4], (C4,), 0.5, 3.0, (), jnp.float32),
        "third_linear": jnp.clip(jnp.exp(jax.random.uniform(streams_of[5], (C3,), jnp.float32, math.log(8.0), math.log(64.0))), 8.0, 64.0),
        "fourth_linear": jnp.clip(jnp.exp(jax.random.uniform(streams_of[6], (C4,), jnp.float32, math.log(8.0), math.log(64.0))), 8.0, 64.0),
    }


EPS = 1e-06

def conv_rows(padded, weight, bias):
    stacks, rows_in, width, chans = padded.shape
    height = rows_in - 2
    widened = jnp.pad(padded, ((0, 0), (0, 0), (1, 1), (0, 0)))
    total = jnp.zeros((stacks * height * width, weight.shape[3]), jnp.float32)
    for offset in range(3):
        strip = widened[:, offset:offset + height]
        joined = jnp.concatenate([strip[:, :, 0:width], strip[:, :, 1:width + 1], strip[:, :, 2:width + 2]], axis=3)
        total = total + jnp.dot(joined.reshape(-1, 3 * chans), weight[offset].reshape(3 * chans, -1), preferred_element_type=jnp.float32)
    return total.reshape(stacks, height, width, -1) + bias.astype(jnp.float32)

def conv_back(padded, weight):
    height = padded.shape[0] - 2
    width = padded.shape[1]
    outputs = weight.shape[3]
    widened = jnp.pad(padded, ((0, 0), (1, 1), (0, 0)))
    total = jnp.zeros((height * width, weight.shape[2]), jnp.float32)
    for offset in range(3):
        strip = widened[2 - offset:2 - offset + height]
        joined = jnp.concatenate([strip[:, 2 - step:2 - step + width] for step in range(3)], axis=2)
        flipped = jnp.transpose(weight[offset], (0, 2, 1)).reshape(3 * outputs, -1)
        total = total + jnp.dot(joined.reshape(-1, 3 * outputs), flipped, preferred_element_type=jnp.float32)
    return total.reshape(height, width, -1)

def silu_grad(pre):
    sig = jax.nn.sigmoid(pre)
    return sig * (1.0 + pre * (1.0 - sig))

def lpips_grad(first, second, linear):
    chans = first.shape[-1]
    scale_first = jnp.sqrt(lax.optimization_barrier(jnp.sum(first * first, -1, keepdims=True)) + chans * EPS)
    scale_second = jnp.sqrt(lax.optimization_barrier(jnp.sum(second * second, -1, keepdims=True)) + chans * EPS)
    unit_first = first / scale_first
    weighted = linear * (unit_first - second / scale_second)
    return 2.0 * (weighted - unit_first * lax.optimization_barrier(jnp.sum(weighted * unit_first, -1, keepdims=True))) / scale_first

def pool_mean(field):
    stacks, height, width, chans = field.shape
    blocks = field.astype(jnp.float32).reshape(stacks, height // 2, 2, width // 2, 2, chans)
    return lax.optimization_barrier(jnp.mean(blocks, axis=(2, 4)))

def upsample(field):
    height, width, chans = field.shape
    grown = jnp.broadcast_to(field[:, None, :, None, :], (height, 2, width, 2, chans))
    return 0.25 * grown.reshape(2 * height, 2 * width, chans)

def reference(images, third_weight, third_bias, fourth_weight, fourth_bias, third_linear, fourth_linear):
    pre3 = conv_rows(jnp.pad(images, ((0, 0), (1, 1), (0, 0), (0, 0))), third_weight, third_bias)
    act3 = jax.nn.silu(pre3).astype(jnp.bfloat16)
    pooled = pool_mean(act3).astype(jnp.bfloat16)
    pre4 = conv_rows(jnp.pad(pooled, ((0, 0), (1, 1), (0, 0), (0, 0))), fourth_weight, fourth_bias)
    act4 = jax.nn.silu(pre4)
    grad4 = (lpips_grad(act4[0], act4[1], fourth_linear) * silu_grad(pre4[0])).astype(jnp.bfloat16)
    back4 = conv_back(jnp.pad(grad4, ((1, 1), (0, 0), (0, 0))), fourth_weight)
    near = lpips_grad(act3[0].astype(jnp.float32), act3[1].astype(jnp.float32), third_linear)
    grad3 = ((upsample(back4) + near) * silu_grad(pre3[0])).astype(jnp.bfloat16)
    return conv_back(jnp.pad(grad3, ((1, 1), (0, 0), (0, 0))), third_weight)
```

```python
import functools
import jax
import jax.numpy as jnp
from jax import lax
from jax.experimental import pallas as pl
from jax.experimental.pallas import tpu as pltpu
from jax.sharding import PartitionSpec as P

EPS = 1e-06
F32 = jnp.float32
BF16 = jnp.bfloat16
MESH = pl.DeviceIdType.MESH


def sigmoid(v):
    return 0.5 * jnp.tanh(0.5 * v) + 0.5


def silu_grad(pre, sig):
    return sig * (1.0 + pre * (1.0 - sig))


def lpips_grad(first, second, linear):
    chans = first.shape[-1]
    inv_first = lax.rsqrt(jnp.sum(first * first, -1, keepdims=True) + chans * EPS)
    inv_second = lax.rsqrt(jnp.sum(second * second, -1, keepdims=True) + chans * EPS)
    unit = first * inv_first
    weighted = linear * (unit - second * inv_second)
    along = jnp.sum(weighted * unit, -1, keepdims=True)
    return (weighted - unit * along) * (2.0 * inv_first)


def expand(ref, lead, chans):
    centre = ref[lead + (slice(None), pl.ds(chans, chans))]
    width = centre.shape[0]
    wide = centre.astype(F32)
    col = lax.broadcasted_iota(jnp.int32, wide.shape, 0)
    before = jnp.where(col == 0, 0.0, pltpu.roll(wide, 1, 0)).astype(BF16)
    after = jnp.where(col == width - 1, 0.0, pltpu.roll(wide, width - 1, 0)).astype(BF16)
    ref[lead + (slice(None), pl.ds(0, chans))] = before
    ref[lead + (slice(None), pl.ds(2 * chans, chans))] = after


def dot_nt(a, b):
    return lax.dot_general(a, b, (((1,), (1,)), ((), ())), preferred_element_type=F32)


def kernel(
    n, img, w3h, w4h, b3, b4, l3, l4, out,
    x3, w3, w4, p3, g4, g3, gate, near, fold, grow, outv,
    local_sem, out_sem, send_sem, recv_sem,
):
    rows = img.shape[1]
    half = rows // 2
    c3 = w3.shape[3]
    c4 = w4.shape[3]
    width = img.shape[2]
    mid = width // 2
    group = lax.axis_index("groups")
    pos = lax.axis_index("rows")
    has_up = pos > 0
    has_down = pos < n - 1

    in_copies = [
        pltpu.make_async_copy(img, x3.at[:, pl.ds(1, rows), :, pl.ds(c3, c3)], local_sem.at[0]),
        pltpu.make_async_copy(w3h, w3, local_sem.at[1]),
        pltpu.make_async_copy(w4h, w4, local_sem.at[2]),
    ]
    for copy in in_copies:
        copy.start()

    barrier = pltpu.get_barrier_semaphore()

    @pl.when(has_up)
    def _():
        pl.semaphore_signal(barrier, inc=1, device_id=(group, pos - 1), device_id_type=MESH)

    @pl.when(has_down)
    def _():
        pl.semaphore_signal(barrier, inc=1, device_id=(group, pos + 1), device_id_type=MESH)

    pl.semaphore_wait(barrier, has_up.astype(jnp.int32) + has_down.astype(jnp.int32))

    def halo(which, src_last, dst_first, src_first, dst_last):
        down = pltpu.make_async_remote_copy(
            src_ref=src_last, dst_ref=dst_first,
            send_sem=send_sem.at[which, 0], recv_sem=recv_sem.at[which, 0],
            device_id=(group, pos + 1), device_id_type=MESH,
        )
        up = pltpu.make_async_remote_copy(
            src_ref=src_first, dst_ref=dst_last,
            send_sem=send_sem.at[which, 1], recv_sem=recv_sem.at[which, 1],
            device_id=(group, pos - 1), device_id_type=MESH,
        )

        def start():
            @pl.when(has_down)
            def _():
                down.start()

            @pl.when(has_up)
            def _():
                up.start()

        def arrive():
            @pl.when(has_up)
            def _():
                down.wait_recv()

            @pl.when(jnp.logical_not(has_up))
            def _():
                dst_first[...] = jnp.zeros(dst_first.shape, BF16)

            @pl.when(has_down)
            def _():
                up.wait_recv()

            @pl.when(jnp.logical_not(has_down))
            def _():
                dst_last[...] = jnp.zeros(dst_last.shape, BF16)

        def sent():
            @pl.when(has_down)
            def _():
                down.wait_send()

            @pl.when(has_up)
            def _():
                up.wait_send()

        return start, arrive, sent

    at3 = lambda row: x3.at[:, row, :, pl.ds(c3, c3)]
    atp = lambda row: p3.at[:, row, :, pl.ds(c3, c3)]
    at4 = lambda row: g4.at[row, :, pl.ds(c4, c4)]
    atg = lambda row: g3.at[row, :, pl.ds(c3, c3)]
    halos = [
        halo(0, img.at[:, rows - 1], at3(0), img.at[:, 0], at3(rows + 1)),
        halo(1, atp(half), atp(0), atp(1), atp(half + 1)),
        halo(2, at4(half), at4(0), at4(1), at4(half + 1)),
        halo(3, atg(rows), atg(0), atg(1), atg(rows + 1)),
    ]
    halos[0][0]()
    in_copies[0].wait()

    @pl.loop(1, rows + 1)
    def _(row):
        for m in range(2):
            expand(x3, (m, row), c3)

    in_copies[1].wait()

    def third(pair):
        bias = b3[...]
        linear = l3[...]
        kern = w3[...].reshape(9 * c3, c3)
        acts = []
        for j in range(2):
            row = 2 * pair + j
            pres = []
            for m in range(2):
                lhs = jnp.concatenate([x3[m, row + a] for a in range(3)], axis=1)
                pres.append(jnp.dot(lhs, kern, preferred_element_type=F32) + bias)
            sigs = [sigmoid(v) for v in pres]
            act = [(v * s).astype(BF16).astype(F32) for v, s in zip(pres, sigs)]
            slope = silu_grad(pres[0], sigs[0])
            gate[row] = slope
            near[row] = lpips_grad(act[0], act[1], linear) * slope
            acts.append(act)
        for m in range(2):
            total = acts[0][m] + acts[1][m]
            for k in range(c3 // 128):
                fold[m, k] = total[:, k * 128 : (k + 1) * 128]
            for k in range(c3 // 128):
                even = fold[m, k, pl.ds(0, mid, 2), :]
                odd = fold[m, k, pl.ds(1, mid, 2), :]
                p3[m, pair + 1, :, pl.ds(c3 + k * 128, 128)] = (0.25 * (even + odd)).astype(BF16)
            expand(p3, (m, pair + 1), c3)

    pl.loop(1, half - 1)(third)
    halos[0][1]()
    for m in range(2):
        expand(x3, (m, 0), c3)
        expand(x3, (m, rows + 1), c3)
    pl.loop(0, 2)(lambda i: third(i * (half - 1)))
    halos[1][0]()

    in_copies[2].wait()

    def fourth(one, two):
        kern = w4[...].reshape(9 * c3, c4)
        pres = []
        for m in range(2):
            lhs = jnp.concatenate(
                [
                    jnp.concatenate([p3[m, row + a] for a in range(3)], axis=1)
                    for row in (one, two)
                ],
                axis=0,
            )
            pres.append(jnp.dot(lhs, kern, preferred_element_type=F32) + b4[...])
        sigs = [sigmoid(v) for v in pres]
        slope = silu_grad(pres[0], sigs[0])
        grad = lpips_grad(pres[0] * sigs[0], pres[1] * sigs[1], l4[...]) * slope
        grad = grad.astype(BF16)
        for k, row in enumerate((one, two)):
            g4[row + 1, :, pl.ds(c4, c4)] = grad[k * mid : (k + 1) * mid]

    pairs = [(row, row + 1) for row in range(1, half - 1, 2)]
    for one, two in pairs:
        fourth(one, two)
    halos[1][1]()
    for m in range(2):
        expand(p3, (m, 0), c3)
        expand(p3, (m, half + 1), c3)
    fourth(0, half - 1)
    halos[2][0]()

    @pl.loop(1, half + 1)
    def _(row):
        expand(g4, (row,), c4)

    def third_grad(one, two):
        total = None
        for a in range(3):
            for b in range(3):
                part = pl.ds((2 - b) * c4, c4)
                lhs = jnp.concatenate([g4[row + 2 - a, :, part] for row in (one, two)], axis=0)
                term = dot_nt(lhs, w4[a, b])
                total = term if total is None else total + term
        total = 0.25 * total
        for k, row in enumerate((one, two)):
            for h in range(c3 // 128):
                piece = total[k * mid : (k + 1) * mid, h * 128 : (h + 1) * 128]
                grow[k, h, pl.ds(0, mid, 2), :] = piece
                grow[k, h, pl.ds(1, mid, 2), :] = piece
            for j in range(2):
                for h in range(c3 // 128):
                    lanes = pl.ds(h * 128, 128)
                    value = grow[k, h] * gate[2 * row + j, :, lanes] + near[2 * row + j, :, lanes]
                    g3[2 * row + j + 1, :, pl.ds(c3 + h * 128, 128)] = value.astype(BF16)

    for one, two in pairs:
        third_grad(one, two)
    halos[2][1]()
    expand(g4, (0,), c4)
    expand(g4, (half + 1,), c4)
    third_grad(0, half - 1)
    halos[3][0]()

    @pl.loop(1, rows + 1)
    def _(row):
        expand(g3, (row,), c3)

    def result(one, two):
        total = None
        for a in range(3):
            for b in range(3):
                part = pl.ds((2 - b) * c3, c3)
                lhs = jnp.concatenate([g3[row + 2 - a, :, part] for row in (one, two)], axis=0)
                term = dot_nt(lhs, w3[a, b])
                total = term if total is None else total + term
        outv[one] = total[:width]
        outv[two] = total[width:]

    pl.loop(0, half - 1)(lambda i: result(2 * i + 1, 2 * i + 2))
    inner = pltpu.make_async_copy(
        outv.at[pl.ds(1, rows - 2)], out.at[pl.ds(1, rows - 2)], out_sem.at[0]
    )
    inner.start()
    halos[3][1]()
    expand(g3, (0,), c3)
    expand(g3, (rows + 1,), c3)
    result(0, rows - 1)
    first = pltpu.make_async_copy(outv.at[0], out.at[0], out_sem.at[1])
    last = pltpu.make_async_copy(outv.at[rows - 1], out.at[rows - 1], out_sem.at[2])
    first.start()
    last.start()
    for each in halos:
        each[2]()
    inner.wait()
    first.wait()
    last.wait()


def local(
    images, third_weight, third_bias, fourth_weight, fourth_bias, third_linear, fourth_linear
):
    n = lax.axis_size("rows")
    _, rows, width, c3 = images.shape
    c4 = fourth_weight.shape[3]
    half, mid = rows // 2, width // 2
    anywhere = pl.BlockSpec(memory_space=pl.ANY)
    vmem = pl.BlockSpec(memory_space=pltpu.VMEM)
    return pl.pallas_call(
        functools.partial(kernel, n),
        out_shape=jax.ShapeDtypeStruct((rows, width, c3), F32),
        in_specs=[anywhere] * 3 + [vmem] * 4,
        out_specs=anywhere,
        scratch_shapes=[
            pltpu.VMEM((2, rows + 2, width, 3 * c3), BF16),
            pltpu.VMEM(third_weight.shape, BF16),
            pltpu.VMEM(fourth_weight.shape, BF16),
            pltpu.VMEM((2, half + 2, mid, 3 * c3), BF16),
            pltpu.VMEM((half + 2, mid, 3 * c4), BF16),
            pltpu.VMEM((rows + 2, width, 3 * c3), BF16),
            pltpu.VMEM((rows, width, c3), F32),
            pltpu.VMEM((rows, width, c3), F32),
            pltpu.VMEM((2, c3 // 128, width, 128), F32),
            pltpu.VMEM((2, c3 // 128, width, 128), F32),
            pltpu.VMEM((rows, width, c3), F32),
            pltpu.SemaphoreType.DMA((3,)),
            pltpu.SemaphoreType.DMA((3,)),
            pltpu.SemaphoreType.DMA((4, 2)),
            pltpu.SemaphoreType.DMA((4, 2)),
        ],
        compiler_params=pltpu.CompilerParams(
            collective_id=0, has_side_effects=True, vmem_limit_bytes=56 * 2**20
        ),
    )(
        images, third_weight, fourth_weight,
        third_bias.reshape(1, c3), fourth_bias.reshape(1, c4),
        third_linear.reshape(1, c3), fourth_linear.reshape(1, c4),
    )


def solution(mesh):
    return jax.shard_map(
        local,
        mesh=mesh,
        in_specs=(P(None, ("groups", "rows"), None, None), P(), P(), P(), P(), P(), P()),
        out_specs=P(("groups", "rows"), None, None),
        check_vma=False,
    )
```

```python
import functools
import jax
import jax.numpy as jnp
from jax import lax
from jax.experimental import pallas as pl
from jax.experimental.pallas import tpu as pltpu
from jax.sharding import PartitionSpec as P

EPS = 1e-06
F32 = jnp.float32
BF16 = jnp.bfloat16
MESH = pl.DeviceIdType.MESH


def sigmoid(v):
    return 0.5 * jnp.tanh(0.5 * v) + 0.5


def silu_grad(pre, sig):
    return sig * (1.0 + pre * (1.0 - sig))


def lpips_grad(first, second, linear):
    chans = first.shape[-1]
    inv_first = lax.rsqrt(jnp.sum(first * first, -1, keepdims=True) + chans * EPS)
    inv_second = lax.rsqrt(jnp.sum(second * second, -1, keepdims=True) + chans * EPS)
    unit = first * inv_first
    weighted = linear * (unit - second * inv_second)
    along = jnp.sum(weighted * unit, -1, keepdims=True)
    return (weighted - unit * along) * (2.0 * inv_first)


def expand(ref, lead, chans):
    centre = ref[lead + (slice(None), pl.ds(chans, chans))]
    width = centre.shape[0]
    wide = centre.astype(F32)
    col = lax.broadcasted_iota(jnp.int32, wide.shape, 0)
    before = jnp.where(col == 0, 0.0, pltpu.roll(wide, 1, 0)).astype(BF16)
    after = jnp.where(col == width - 1, 0.0, pltpu.roll(wide, width - 1, 0)).astype(BF16)
    ref[lead + (slice(None), pl.ds(0, chans))] = before
    ref[lead + (slice(None), pl.ds(2 * chans, chans))] = after


def dot_nt(a, b):
    return lax.dot_general(a, b, (((1,), (1,)), ((), ())), preferred_element_type=F32)


def kernel(
    n, img, w3h, w4h, b3, b4, l3, l4, out,
    x3, w3, w4, p3, g4, g3, gate, near, fold, grow, outv, part3, acts3, part4, partb,
    local_sem, out_sem, send_sem, recv_sem,
):
    rows = img.shape[1]
    half = rows // 2
    c3 = w3.shape[3]
    c4 = w4.shape[3]
    width = img.shape[2]
    mid = width // 2
    group = lax.axis_index("groups")
    pos = lax.axis_index("rows")
    has_up = pos > 0
    has_down = pos < n - 1

    in_copies = [
        pltpu.make_async_copy(img, x3.at[:, pl.ds(1, rows), :, pl.ds(c3, c3)], local_sem.at[0]),
        pltpu.make_async_copy(w3h, w3, local_sem.at[1]),
        pltpu.make_async_copy(w4h, w4, local_sem.at[2]),
    ]
    for copy in in_copies:
        copy.start()

    barrier = pltpu.get_barrier_semaphore()

    @pl.when(has_up)
    def _():
        pl.semaphore_signal(barrier, inc=1, device_id=(group, pos - 1), device_id_type=MESH)

    @pl.when(has_down)
    def _():
        pl.semaphore_signal(barrier, inc=1, device_id=(group, pos + 1), device_id_type=MESH)

    pl.semaphore_wait(barrier, has_up.astype(jnp.int32) + has_down.astype(jnp.int32))

    def halo(which, src_last, dst_first, src_first, dst_last):
        down = pltpu.make_async_remote_copy(
            src_ref=src_last, dst_ref=dst_first,
            send_sem=send_sem.at[which, 0], recv_sem=recv_sem.at[which, 0],
            device_id=(group, pos + 1), device_id_type=MESH,
        )
        up = pltpu.make_async_remote_copy(
            src_ref=src_first, dst_ref=dst_last,
            send_sem=send_sem.at[which, 1], recv_sem=recv_sem.at[which, 1],
            device_id=(group, pos - 1), device_id_type=MESH,
        )

        def start():
            @pl.when(has_down)
            def _():
                down.start()

            @pl.when(has_up)
            def _():
                up.start()

        def arrive():
            @pl.when(has_up)
            def _():
                down.wait_recv()

            @pl.when(jnp.logical_not(has_up))
            def _():
                dst_first[...] = jnp.zeros(dst_first.shape, BF16)

            @pl.when(has_down)
            def _():
                up.wait_recv()

            @pl.when(jnp.logical_not(has_down))
            def _():
                dst_last[...] = jnp.zeros(dst_last.shape, BF16)

        def sent():
            @pl.when(has_down)
            def _():
                down.wait_send()

            @pl.when(has_up)
            def _():
                up.wait_send()

        return start, arrive, sent

    at3 = lambda row: x3.at[:, row, :, pl.ds(c3, c3)]
    atp = lambda row: p3.at[:, row, :, pl.ds(c3, c3)]
    at4 = lambda row: g4.at[row, :, pl.ds(c4, c4)]
    atg = lambda row: g3.at[row, :, pl.ds(c3, c3)]
    halos = [
        halo(0, img.at[:, rows - 1], at3(0), img.at[:, 0], at3(rows + 1)),
        halo(1, atp(half), atp(0), atp(1), atp(half + 1)),
        halo(2, at4(half), at4(0), at4(1), at4(half + 1)),
        halo(3, atg(rows), atg(0), atg(1), atg(rows + 1)),
    ]
    halos[0][0]()
    in_copies[0].wait()

    @pl.loop(1, rows + 1)
    def _(row):
        for m in range(2):
            expand(x3, (m, row), c3)

    in_copies[1].wait()

    def pool(m, pair, total):
        for k in range(c3 // 128):
            fold[m, k] = total[:, k * 128 : (k + 1) * 128]
        for k in range(c3 // 128):
            even = fold[m, k, pl.ds(0, mid, 2), :]
            odd = fold[m, k, pl.ds(1, mid, 2), :]
            p3[m, pair + 1, :, pl.ds(c3 + k * 128, 128)] = (0.25 * (even + odd)).astype(BF16)

    edges = [(0, 0, 1, (1, 2), 0), (1, rows - 1, rows - 2, (0, 1), 2)]

    def third_early(edge, row, partner, taps, _):
        kern = w3[...].reshape(9 * c3, c3)
        some = w3[pl.ds(taps[0], 2)].reshape(6 * c3, c3)
        pres = []
        for m in range(2):
            lhs = jnp.concatenate([x3[m, partner + a] for a in range(3)], axis=1)
            pres.append(jnp.dot(lhs, kern, preferred_element_type=F32) + b3[...])
            lhs = jnp.concatenate([x3[m, row + a] for a in taps], axis=1)
            part3[edge, m] = jnp.dot(lhs, some, preferred_element_type=F32) + b3[...]
        sigs = [sigmoid(v) for v in pres]
        act = [(v * s).astype(BF16).astype(F32) for v, s in zip(pres, sigs)]
        slope = silu_grad(pres[0], sigs[0])
        gate[partner] = slope
        near[partner] = lpips_grad(act[0], act[1], l3[...]) * slope
        for m in range(2):
            acts3[edge, m] = act[m]

    def third_late(edge, row, partner, taps, tap):
        kern = w3[tap].reshape(3 * c3, c3)
        for m in range(2):
            pre = part3[edge, m] + jnp.dot(
                x3[m, row + tap], kern, preferred_element_type=F32
            )
            act = (pre * sigmoid(pre)).astype(BF16).astype(F32)
            pool(m, row // 2, act + acts3[edge, m])
            acts3[edge, m] = act
            if m == 0:
                part3[edge, m] = pre

    def third_near(edge, row, partner, taps, tap):
        pre = part3[edge, 0]
        slope = silu_grad(pre, sigmoid(pre))
        gate[row] = slope
        near[row] = lpips_grad(acts3[edge, 0], acts3[edge, 1], l3[...]) * slope
        for m in range(2):
            expand(p3, (m, row // 2 + 1), c3)

    def third(pair):
        bias = b3[...]
        linear = l3[...]
        kern = w3[...].reshape(9 * c3, c3)
        acts = []
        for j in range(2):
            row = 2 * pair + j
            pres = []
            for m in range(2):
                lhs = jnp.concatenate([x3[m, row + a] for a in range(3)], axis=1)
                pres.append(jnp.dot(lhs, kern, preferred_element_type=F32) + bias)
            sigs = [sigmoid(v) for v in pres]
            act = [(v * s).astype(BF16).astype(F32) for v, s in zip(pres, sigs)]
            slope = silu_grad(pres[0], sigs[0])
            gate[row] = slope
            near[row] = lpips_grad(act[0], act[1], linear) * slope
            acts.append(act)
        for m in range(2):
            total = acts[0][m] + acts[1][m]
            pool(m, pair, total)
            expand(p3, (m, pair + 1), c3)

    pl.loop(1, half - 1)(third)
    for edge in edges:
        third_early(*edge)
    halos[0][1]()
    for m in range(2):
        expand(x3, (m, 0), c3)
        expand(x3, (m, rows + 1), c3)
    for edge in edges:
        third_late(*edge)
    halos[1][0]()
    for edge in edges:
        third_near(*edge)

    in_copies[2].wait()

    def fourth(one, two):
        kern = w4[...].reshape(9 * c3, c4)
        pres = []
        for m in range(2):
            lhs = jnp.concatenate(
                [
                    jnp.concatenate([p3[m, row + a] for a in range(3)], axis=1)
                    for row in (one, two)
                ],
                axis=0,
            )
            pres.append(jnp.dot(lhs, kern, preferred_element_type=F32) + b4[...])
        fourth_grad(pres, one, two)

    def fourth_grad(pres, one, two):
        sigs = [sigmoid(v) for v in pres]
        slope = silu_grad(pres[0], sigs[0])
        grad = lpips_grad(pres[0] * sigs[0], pres[1] * sigs[1], l4[...]) * slope
        grad = grad.astype(BF16)
        for k, row in enumerate((one, two)):
            g4[row + 1, :, pl.ds(c4, c4)] = grad[k * mid : (k + 1) * mid]

    coarse = [(0, 0, (1, 2), 0), (1, half - 1, (0, 1), 2)]

    def fourth_early(edge, row, taps, _):
        kern = w4[pl.ds(taps[0], 2)].reshape(6 * c3, c4)
        lhs = jnp.concatenate(
            [jnp.concatenate([p3[m, row + a] for a in taps], axis=1) for m in range(2)], axis=0
        )
        part4[edge] = jnp.dot(lhs, kern, preferred_element_type=F32) + b4[...]

    def fourth_late():
        whole = []
        for edge, row, _, tap in coarse:
            lhs = jnp.concatenate([p3[m, row + tap] for m in range(2)], axis=0)
            kern = w4[tap].reshape(3 * c3, c4)
            whole.append(part4[edge] + jnp.dot(lhs, kern, preferred_element_type=F32))
        pres = [
            jnp.concatenate([v[m * mid : (m + 1) * mid] for v in whole], axis=0)
            for m in range(2)
        ]
        fourth_grad(pres, 0, half - 1)

    pairs = [(row, row + 1) for row in range(1, half - 1, 2)]
    for one, two in pairs:
        fourth(one, two)
    for edge in coarse:
        fourth_early(*edge)
    halos[1][1]()
    for m in range(2):
        expand(p3, (m, 0), c3)
        expand(p3, (m, half + 1), c3)
    fourth_late()
    halos[2][0]()

    @pl.loop(1, half + 1)
    def _(row):
        expand(g4, (row,), c4)

    def third_grad(one, two):
        total = None
        for a in range(3):
            for b in range(3):
                part = pl.ds((2 - b) * c4, c4)
                lhs = jnp.concatenate([g4[row + 2 - a, :, part] for row in (one, two)], axis=0)
                term = dot_nt(lhs, w4[a, b])
                total = term if total is None else total + term
        third_value(0.25 * total, one, two)

    def third_value(total, one, two):
        for k, row in enumerate((one, two)):
            for h in range(c3 // 128):
                piece = total[k * mid : (k + 1) * mid, h * 128 : (h + 1) * 128]
                grow[k, h, pl.ds(0, mid, 2), :] = piece
                grow[k, h, pl.ds(1, mid, 2), :] = piece
            for j in range(2):
                for h in range(c3 // 128):
                    lanes = pl.ds(h * 128, 128)
                    value = grow[k, h] * gate[2 * row + j, :, lanes] + near[2 * row + j, :, lanes]
                    g3[2 * row + j + 1, :, pl.ds(c3 + h * 128, 128)] = value.astype(BF16)

    for one, two in pairs:
        third_grad(one, two)

    def back(ref, kern, chans, row, taps):
        total = None
        for a in taps:
            for b in range(3):
                lhs = ref[row + 2 - a, :, pl.ds((2 - b) * chans, chans)]
                term = dot_nt(lhs, kern[a, b])
                total = term if total is None else total + term
        return total

    partb[0] = back(g4, w4, c4, 0, (0, 1))
    partb[1] = back(g4, w4, c4, half - 1, (1, 2))
    halos[2][1]()
    expand(g4, (0,), c4)
    expand(g4, (half + 1,), c4)
    ends = [
        partb[0] + back(g4, w4, c4, 0, (2,)),
        partb[1] + back(g4, w4, c4, half - 1, (0,)),
    ]
    third_value(0.25 * jnp.concatenate(ends, axis=0), 0, half - 1)
    halos[3][0]()

    @pl.loop(1, rows + 1)
    def _(row):
        expand(g3, (row,), c3)

    def result(one, two):
        total = None
        for a in range(3):
            for b in range(3):
                part = pl.ds((2 - b) * c3, c3)
                lhs = jnp.concatenate([g3[row + 2 - a, :, part] for row in (one, two)], axis=0)
                term = dot_nt(lhs, w3[a, b])
                total = term if total is None else total + term
        outv[one] = total[:width]
        outv[two] = total[width:]

    pl.loop(0, half - 1)(lambda i: result(2 * i + 1, 2 * i + 2))
    inner = pltpu.make_async_copy(
        outv.at[pl.ds(1, rows - 2)], out.at[pl.ds(1, rows - 2)], out_sem.at[0]
    )
    inner.start()
    outv[0] = back(g3, w3, c3, 0, (0, 1))
    outv[rows - 1] = back(g3, w3, c3, rows - 1, (1, 2))
    halos[3][1]()
    expand(g3, (0,), c3)
    expand(g3, (rows + 1,), c3)
    outv[0] = outv[0] + back(g3, w3, c3, 0, (2,))
    outv[rows - 1] = outv[rows - 1] + back(g3, w3, c3, rows - 1, (0,))
    first = pltpu.make_async_copy(outv.at[0], out.at[0], out_sem.at[1])
    last = pltpu.make_async_copy(outv.at[rows - 1], out.at[rows - 1], out_sem.at[2])
    first.start()
    last.start()
    for each in halos:
        each[2]()
    inner.wait()
    first.wait()
    last.wait()


def local(
    images, third_weight, third_bias, fourth_weight, fourth_bias, third_linear, fourth_linear
):
    n = lax.axis_size("rows")
    _, rows, width, c3 = images.shape
    c4 = fourth_weight.shape[3]
    half, mid = rows // 2, width // 2
    anywhere = pl.BlockSpec(memory_space=pl.ANY)
    vmem = pl.BlockSpec(memory_space=pltpu.VMEM)
    return pl.pallas_call(
        functools.partial(kernel, n),
        out_shape=jax.ShapeDtypeStruct((rows, width, c3), F32),
        in_specs=[anywhere] * 3 + [vmem] * 4,
        out_specs=anywhere,
        scratch_shapes=[
            pltpu.VMEM((2, rows + 2, width, 3 * c3), BF16),
            pltpu.VMEM(third_weight.shape, BF16),
            pltpu.VMEM(fourth_weight.shape, BF16),
            pltpu.VMEM((2, half + 2, mid, 3 * c3), BF16),
            pltpu.VMEM((half + 2, mid, 3 * c4), BF16),
            pltpu.VMEM((rows + 2, width, 3 * c3), BF16),
            pltpu.VMEM((rows, width, c3), F32),
            pltpu.VMEM((rows, width, c3), F32),
            pltpu.VMEM((2, c3 // 128, width, 128), F32),
            pltpu.VMEM((2, c3 // 128, width, 128), F32),
            pltpu.VMEM((rows, width, c3), F32),
            pltpu.VMEM((2, 2, width, c3), F32),
            pltpu.VMEM((2, 2, width, c3), F32),
            pltpu.VMEM((2, 2 * mid, c4), F32),
            pltpu.VMEM((2, mid, c3), F32),
            pltpu.SemaphoreType.DMA((3,)),
            pltpu.SemaphoreType.DMA((3,)),
            pltpu.SemaphoreType.DMA((4, 2)),
            pltpu.SemaphoreType.DMA((4, 2)),
        ],
        compiler_params=pltpu.CompilerParams(
            collective_id=0, has_side_effects=True, vmem_limit_bytes=56 * 2**20
        ),
    )(
        images, third_weight, fourth_weight,
        third_bias.reshape(1, c3), fourth_bias.reshape(1, c4),
        third_linear.reshape(1, c3), fourth_linear.reshape(1, c4),
    )


def solution(mesh):
    return jax.shard_map(
        local,
        mesh=mesh,
        in_specs=(P(None, ("groups", "rows"), None, None), P(), P(), P(), P(), P(), P()),
        out_specs=P(("groups", "rows"), None, None),
        check_vma=False,
    )
```

```python
import functools
import jax
import jax.numpy as jnp
from jax import lax
from jax.experimental import pallas as pl
from jax.experimental.pallas import tpu as pltpu
from jax.sharding import PartitionSpec as P

EPS = 1e-06
F32 = jnp.float32
BF16 = jnp.bfloat16
MESH = pl.DeviceIdType.MESH


def sigmoid(v):
    return 0.5 * jnp.tanh(0.5 * v) + 0.5


def silu_grad(pre, sig):
    return sig * (1.0 + pre * (1.0 - sig))


def lpips_grad(first, second, linear):
    chans = first.shape[-1]
    inv_first = lax.rsqrt(jnp.sum(first * first, -1, keepdims=True) + chans * EPS)
    inv_second = lax.rsqrt(jnp.sum(second * second, -1, keepdims=True) + chans * EPS)
    unit = first * inv_first
    weighted = linear * (unit - second * inv_second)
    along = jnp.sum(weighted * unit, -1, keepdims=True)
    return (weighted - unit * along) * (2.0 * inv_first)


def expand(ref, lead, chans):
    centre = ref[lead + (slice(None), pl.ds(chans, chans))]
    width = centre.shape[0]
    wide = centre.astype(F32)
    col = lax.broadcasted_iota(jnp.int32, wide.shape, 0)
    before = jnp.where(col == 0, 0.0, pltpu.roll(wide, 1, 0)).astype(BF16)
    after = jnp.where(col == width - 1, 0.0, pltpu.roll(wide, width - 1, 0)).astype(BF16)
    ref[lead + (slice(None), pl.ds(0, chans))] = before
    ref[lead + (slice(None), pl.ds(2 * chans, chans))] = after


def dot_nt(a, b):
    return lax.dot_general(a, b, (((1,), (1,)), ((), ())), preferred_element_type=F32)


def kernel(
    n, img, w3h, w4h, b3, b4, l3, l4, out,
    x3, w3, w4, p3, g4, g3, gate, near, fold, grow, outv, part3, acts3, part4, partb,
    local_sem, out_sem, send_sem, recv_sem,
):
    rows = img.shape[1]
    half = rows // 2
    c3 = w3.shape[3]
    c4 = w4.shape[3]
    width = img.shape[2]
    mid = width // 2
    group = lax.axis_index("groups")
    pos = lax.axis_index("rows")
    has_up = pos > 0
    has_down = pos < n - 1

    in_copies = [
        pltpu.make_async_copy(img, x3.at[:, pl.ds(1, rows), :, pl.ds(c3, c3)], local_sem.at[0]),
        pltpu.make_async_copy(w3h, w3, local_sem.at[1]),
        pltpu.make_async_copy(w4h, w4, local_sem.at[2]),
    ]
    for copy in in_copies:
        copy.start()

    barrier = pltpu.get_barrier_semaphore()

    @pl.when(has_up)
    def _():
        pl.semaphore_signal(barrier, inc=1, device_id=(group, pos - 1), device_id_type=MESH)

    @pl.when(has_down)
    def _():
        pl.semaphore_signal(barrier, inc=1, device_id=(group, pos + 1), device_id_type=MESH)

    pl.semaphore_wait(barrier, has_up.astype(jnp.int32) + has_down.astype(jnp.int32))

    def halo(which, src_last, dst_first, src_first, dst_last):
        down = pltpu.make_async_remote_copy(
            src_ref=src_last, dst_ref=dst_first,
            send_sem=send_sem.at[which, 0], recv_sem=recv_sem.at[which, 0],
            device_id=(group, pos + 1), device_id_type=MESH,
        )
        up = pltpu.make_async_remote_copy(
            src_ref=src_first, dst_ref=dst_last,
            send_sem=send_sem.at[which, 1], recv_sem=recv_sem.at[which, 1],
            device_id=(group, pos - 1), device_id_type=MESH,
        )

        def start(edge):
            @pl.when((edge == 1) & has_down)
            def _():
                down.start()

            @pl.when((edge == 0) & has_up)
            def _():
                up.start()

        def arrive(edge):
            @pl.when((edge == 0) & has_up)
            def _():
                down.wait_recv()

            @pl.when((edge == 0) & jnp.logical_not(has_up))
            def _():
                dst_first[...] = jnp.zeros(dst_first.shape, BF16)

            @pl.when((edge == 1) & has_down)
            def _():
                up.wait_recv()

            @pl.when((edge == 1) & jnp.logical_not(has_down))
            def _():
                dst_last[...] = jnp.zeros(dst_last.shape, BF16)

        def sent():
            @pl.when(has_down)
            def _():
                down.wait_send()

            @pl.when(has_up)
            def _():
                up.wait_send()

        return start, arrive, sent

    at3 = lambda row: x3.at[:, row, :, pl.ds(c3, c3)]
    atp = lambda row: p3.at[:, row, :, pl.ds(c3, c3)]
    at4 = lambda row: g4.at[row, :, pl.ds(c4, c4)]
    atg = lambda row: g3.at[row, :, pl.ds(c3, c3)]
    halos = [
        halo(0, img.at[:, rows - 1], at3(0), img.at[:, 0], at3(rows + 1)),
        halo(1, atp(half), atp(0), atp(1), atp(half + 1)),
        halo(2, at4(half), at4(0), at4(1), at4(half + 1)),
        halo(3, atg(rows), atg(0), atg(1), atg(rows + 1)),
    ]
    halos[0][0](0)
    halos[0][0](1)

    def sides(which, body):
        @pl.loop(0, 2)
        def _(i):
            edge = lax.rem(i + 1 + lax.rem(pos, 2), 2)
            halos[which][1](edge)
            body(edge)

    in_copies[0].wait()

    @pl.loop(1, rows + 1)
    def _(row):
        for m in range(2):
            expand(x3, (m, row), c3)

    in_copies[1].wait()

    def pool(m, pair, total):
        for k in range(c3 // 128):
            fold[m, k] = total[:, k * 128 : (k + 1) * 128]
        for k in range(c3 // 128):
            even = fold[m, k, pl.ds(0, mid, 2), :]
            odd = fold[m, k, pl.ds(1, mid, 2), :]
            p3[m, pair + 1, :, pl.ds(c3 + k * 128, 128)] = (0.25 * (even + odd)).astype(BF16)

    edges = [(0, 0, 1, (1, 2), 0), (1, rows - 1, rows - 2, (0, 1), 2)]

    def third_early(edge, row, partner, taps, _):
        kern = w3[...].reshape(9 * c3, c3)
        some = w3[pl.ds(taps[0], 2)].reshape(6 * c3, c3)
        pres = []
        for m in range(2):
            lhs = jnp.concatenate([x3[m, partner + a] for a in range(3)], axis=1)
            pres.append(jnp.dot(lhs, kern, preferred_element_type=F32) + b3[...])
            lhs = jnp.concatenate([x3[m, row + a] for a in taps], axis=1)
            part3[edge, m] = jnp.dot(lhs, some, preferred_element_type=F32) + b3[...]
        sigs = [sigmoid(v) for v in pres]
        act = [(v * s).astype(BF16).astype(F32) for v, s in zip(pres, sigs)]
        slope = silu_grad(pres[0], sigs[0])
        gate[partner] = slope
        near[partner] = lpips_grad(act[0], act[1], l3[...]) * slope
        for m in range(2):
            acts3[edge, m] = act[m]

    def third_late(edge, row, pair, tap):
        kern = w3[tap].reshape(3 * c3, c3)
        for m in range(2):
            pre = part3[edge, m] + jnp.dot(
                x3[m, row + tap], kern, preferred_element_type=F32
            )
            act = (pre * sigmoid(pre)).astype(BF16).astype(F32)
            pool(m, pair, act + acts3[edge, m])
            acts3[edge, m] = act
            part3[edge, m] = pre

    def third_near(edge, row, partner, taps, tap):
        pre = part3[edge, 0]
        slope = silu_grad(pre, sigmoid(pre))
        gate[row] = slope
        near[row] = lpips_grad(acts3[edge, 0], acts3[edge, 1], l3[...]) * slope
        for m in range(2):
            expand(p3, (m, row // 2 + 1), c3)

    def third(pair):
        bias = b3[...]
        linear = l3[...]
        kern = w3[...].reshape(9 * c3, c3)
        acts = []
        for j in range(2):
            row = 2 * pair + j
            pres = []
            for m in range(2):
                lhs = jnp.concatenate([x3[m, row + a] for a in range(3)], axis=1)
                pres.append(jnp.dot(lhs, kern, preferred_element_type=F32) + bias)
            sigs = [sigmoid(v) for v in pres]
            act = [(v * s).astype(BF16).astype(F32) for v, s in zip(pres, sigs)]
            slope = silu_grad(pres[0], sigs[0])
            gate[row] = slope
            near[row] = lpips_grad(act[0], act[1], linear) * slope
            acts.append(act)
        for m in range(2):
            total = acts[0][m] + acts[1][m]
            pool(m, pair, total)
            expand(p3, (m, pair + 1), c3)

    pl.loop(1, half - 1)(third)
    for edge in edges:
        third_early(*edge)

    def third_side(edge):
        for m in range(2):
            expand(x3, (m, edge * (rows + 1)), c3)
        third_late(edge, edge * (rows - 1), edge * (half - 1), 2 * edge)
        halos[1][0](edge)

    sides(0, third_side)
    for edge in edges:
        third_near(*edge)

    in_copies[2].wait()

    def fourth(one, two):
        kern = w4[...].reshape(9 * c3, c4)
        pres = []
        for m in range(2):
            lhs = jnp.concatenate(
                [
                    jnp.concatenate([p3[m, row + a] for a in range(3)], axis=1)
                    for row in (one, two)
                ],
                axis=0,
            )
            pres.append(jnp.dot(lhs, kern, preferred_element_type=F32) + b4[...])
        fourth_grad(pres, one, two)

    def fourth_grad(pres, one, two):
        sigs = [sigmoid(v) for v in pres]
        slope = silu_grad(pres[0], sigs[0])
        grad = lpips_grad(pres[0] * sigs[0], pres[1] * sigs[1], l4[...]) * slope
        grad = grad.astype(BF16)
        for k, row in enumerate((one, two)):
            g4[row + 1, :, pl.ds(c4, c4)] = grad[k * mid : (k + 1) * mid]

    coarse = [(0, 0, (1, 2), 0), (1, half - 1, (0, 1), 2)]

    def fourth_early(edge, row, taps, _):
        kern = w4[pl.ds(taps[0], 2)].reshape(6 * c3, c4)
        lhs = jnp.concatenate(
            [jnp.concatenate([p3[m, row + a] for a in taps], axis=1) for m in range(2)], axis=0
        )
        part4[edge] = jnp.dot(lhs, kern, preferred_element_type=F32) + b4[...]

    def fourth_late():
        whole = []
        for edge, row, _, tap in coarse:
            lhs = jnp.concatenate([p3[m, row + tap] for m in range(2)], axis=0)
            kern = w4[tap].reshape(3 * c3, c4)
            whole.append(part4[edge] + jnp.dot(lhs, kern, preferred_element_type=F32))
        pres = [
            jnp.concatenate([v[m * mid : (m + 1) * mid] for v in whole], axis=0)
            for m in range(2)
        ]
        fourth_grad(pres, 0, half - 1)

    pairs = [(row, row + 1) for row in range(1, half - 1, 2)]
    for one, two in pairs:
        fourth(one, two)
    for edge in coarse:
        fourth_early(*edge)
    halos[1][1](0)
    halos[1][1](1)
    for m in range(2):
        expand(p3, (m, 0), c3)
        expand(p3, (m, half + 1), c3)
    fourth_late()
    halos[2][0](0)
    halos[2][0](1)

    @pl.loop(1, half + 1)
    def _(row):
        expand(g4, (row,), c4)

    def third_grad(one, two):
        total = None
        for a in range(3):
            for b in range(3):
                part = pl.ds((2 - b) * c4, c4)
                lhs = jnp.concatenate([g4[row + 2 - a, :, part] for row in (one, two)], axis=0)
                term = dot_nt(lhs, w4[a, b])
                total = term if total is None else total + term
        third_value(0.25 * total, one, two)

    def third_value(total, *places):
        for k, row in enumerate(places):
            for h in range(c3 // 128):
                piece = total[k * mid : (k + 1) * mid, h * 128 : (h + 1) * 128]
                grow[k, h, pl.ds(0, mid, 2), :] = piece
                grow[k, h, pl.ds(1, mid, 2), :] = piece
            for j in range(2):
                for h in range(c3 // 128):
                    lanes = pl.ds(h * 128, 128)
                    value = grow[k, h] * gate[2 * row + j, :, lanes] + near[2 * row + j, :, lanes]
                    g3[2 * row + j + 1, :, pl.ds(c3 + h * 128, 128)] = value.astype(BF16)

    for one, two in pairs:
        third_grad(one, two)

    def back(ref, kern, chans, row, taps):
        total = None
        for a in taps:
            for b in range(3):
                lhs = ref[row + 2 - a, :, pl.ds((2 - b) * chans, chans)]
                term = dot_nt(lhs, kern[a, b])
                total = term if total is None else total + term
        return total

    partb[0] = back(g4, w4, c4, 0, (0, 1))
    partb[1] = back(g4, w4, c4, half - 1, (1, 2))

    def back_side(edge):
        row = edge * (half - 1)
        expand(g4, (edge * (half + 1),), c4)
        total = partb[edge] + back(g4, w4, c4, row, (2 - 2 * edge,))
        third_value(0.25 * total, row)
        halos[3][0](edge)

    sides(2, back_side)

    @pl.loop(1, rows + 1)
    def _(row):
        expand(g3, (row,), c3)

    def result(one, two):
        total = None
        for a in range(3):
            for b in range(3):
                part = pl.ds((2 - b) * c3, c3)
                lhs = jnp.concatenate([g3[row + 2 - a, :, part] for row in (one, two)], axis=0)
                term = dot_nt(lhs, w3[a, b])
                total = term if total is None else total + term
        outv[one] = total[:width].astype(BF16)
        outv[two] = total[width:].astype(BF16)

    pl.loop(0, half - 1)(lambda i: result(2 * i + 1, 2 * i + 2))
    inner = pltpu.make_async_copy(
        outv.at[pl.ds(1, rows - 2)], out.at[pl.ds(1, rows - 2)], out_sem.at[0]
    )
    inner.start()
    part3[0, 0] = back(g3, w3, c3, 0, (0, 1))
    part3[1, 0] = back(g3, w3, c3, rows - 1, (1, 2))

    def last_side(edge):
        row = edge * (rows - 1)
        expand(g3, (edge * (rows + 1),), c3)
        total = part3[edge, 0] + back(g3, w3, c3, row, (2 - 2 * edge,))
        outv[row] = total.astype(BF16)

    sides(3, last_side)
    first = pltpu.make_async_copy(outv.at[0], out.at[0], out_sem.at[1])
    last = pltpu.make_async_copy(outv.at[rows - 1], out.at[rows - 1], out_sem.at[2])
    first.start()
    last.start()
    for each in halos:
        each[2]()
    inner.wait()
    first.wait()
    last.wait()


def local(
    images, third_weight, third_bias, fourth_weight, fourth_bias, third_linear, fourth_linear
):
    n = lax.axis_size("rows")
    _, rows, width, c3 = images.shape
    c4 = fourth_weight.shape[3]
    half, mid = rows // 2, width // 2
    anywhere = pl.BlockSpec(memory_space=pl.ANY)
    vmem = pl.BlockSpec(memory_space=pltpu.VMEM)
    return pl.pallas_call(
        functools.partial(kernel, n),
        out_shape=jax.ShapeDtypeStruct((rows, width, c3), BF16),
        in_specs=[anywhere] * 3 + [vmem] * 4,
        out_specs=anywhere,
        scratch_shapes=[
            pltpu.VMEM((2, rows + 2, width, 3 * c3), BF16),
            pltpu.VMEM(third_weight.shape, BF16),
            pltpu.VMEM(fourth_weight.shape, BF16),
            pltpu.VMEM((2, half + 2, mid, 3 * c3), BF16),
            pltpu.VMEM((half + 2, mid, 3 * c4), BF16),
            pltpu.VMEM((rows + 2, width, 3 * c3), BF16),
            pltpu.VMEM((rows, width, c3), F32),
            pltpu.VMEM((rows, width, c3), F32),
            pltpu.VMEM((2, c3 // 128, width, 128), F32),
            pltpu.VMEM((2, c3 // 128, width, 128), F32),
            pltpu.VMEM((rows, width, c3), BF16),
            pltpu.VMEM((2, 2, width, c3), F32),
            pltpu.VMEM((2, 2, width, c3), F32),
            pltpu.VMEM((2, 2 * mid, c4), F32),
            pltpu.VMEM((2, mid, c3), F32),
            pltpu.SemaphoreType.DMA((3,)),
            pltpu.SemaphoreType.DMA((3,)),
            pltpu.SemaphoreType.DMA((4, 2)),
            pltpu.SemaphoreType.DMA((4, 2)),
        ],
        compiler_params=pltpu.CompilerParams(
            collective_id=0, has_side_effects=True, vmem_limit_bytes=56 * 2**20
        ),
    )(
        images, third_weight, fourth_weight,
        third_bias.reshape(1, c3), fourth_bias.reshape(1, c4),
        third_linear.reshape(1, c3), fourth_linear.reshape(1, c4),
    ).astype(F32)


def solution(mesh):
    return jax.shard_map(
        local,
        mesh=mesh,
        in_specs=(P(None, ("groups", "rows"), None, None), P(), P(), P(), P(), P(), P()),
        out_specs=P(("groups", "rows"), None, None),
        check_vma=False,
    )
```
